32 devices in a mesh: prow: 8 (over y, x, core), pcol: 4 (over z).
Axes of the slice: x: 2, y: 2, z: 4, core: 2. Of those that a mesh axis runs over, the one named last changes fastest.
Arguments:
- rhs_panel: float32 [2048, 2, 256], P(('prow', 'pcol')), may hold values from -6 to 6
- pivots: int32 [2048], replicated, may hold values from 0 to 2047, each once
- diag_inverse: float32 [2048, 2, 2048], P('pcol'), may hold values from -1 to 2, as said below
- panel_column: float32 [2048, 2, 2048], P('prow', None, 'pcol'), may hold values from -0.09375 to 0.09375
- trailing: float32 [2048, 2, 256], P(('prow', 'pcol')), may hold values from -6 to 6
- derivative: float32 [2048, 2, 256], P('pcol'), may hold values from -4 to 4
Outputs:
- updated: float32 [2048, 2, 256], P(('prow', 'pcol'))
- adjoint_panel: float32 [2048, 2, 256], P('pcol')
- sensitivity: float32 [256], replicated
The draws below stay inside these ranges and needn't reach their ends.
Inputs may be any that keep to these rules, and one draw needn't show every extreme that they name: `diag_inverse`: zero above the diagonal in both parts; diagonal real parts between 0.5 and 1.5. `pivots`: each of 0 to 2047 once.
All inputs are finite; a program needn't handle non-finite values.
Results may differ from the reference program's by a relative error of at most 0.00017.
Values sent between devices are 32-bit elements; how exact they have to be, the bound alone decides.
No kernel may reach another device: no remote copies, remote signals or barrier semaphores. Data moves between devices by JAX's collectives and lax.ppermute only.
A program may use at most 64 MiB of HBM per device.

```python
import math
import jax
import jax.numpy as jnp
from jax import lax

NB = 2048
R = 256
ROWS = 2048


def draw_diag_inverse(key, part):
    key = jax.random.fold_in(key, 11)
    first, second, third = jax.random.split(key, 3)
    row_index = jnp.arange(NB)[:, None]
    col_index = jnp.arange(NB)[None, :]
    lower = row_index > col_index
    onside = row_index == col_index
    offdiag = jnp.clip(jax.random.normal(first, (NB, 2, NB), jnp.float32), -5.0, 5.0)
    diag_real = jax.random.uniform(second, (NB, NB), jnp.float32, 0.7, 1.3)
    diag_imag = jax.random.uniform(third, (NB, NB), jnp.float32, -0.3, 0.3)
    scale_off = 1.0 / math.sqrt(NB)
    real_part = jnp.where(lower, offdiag[:, 0, :] * scale_off, 0.0) + jnp.where(onside, diag_real, 0.0)
    imag_part = jnp.where(lower, offdiag[:, 1, :] * scale_off, 0.0) + jnp.where(onside, diag_imag, 0.0)
    return jnp.stack([real_part, imag_part], axis=1).astype(jnp.float32)


def draw_derivative(key, part):
    key = jax.random.fold_in(key, 12)
    first, second = jax.random.split(key, 2)
    rising = 1.0 + 2.0 * jnp.arange(NB, dtype=jnp.float32) / (NB - 1)
    rough = jnp.exp(jax.random.uniform(second, (NB,), jnp.float32, math.log(0.3), math.log(3.0)))
    values = jnp.clip(jax.random.normal(first, (NB, 2, R), jnp.float32), -5.0, 5.0)
    factor = rising * rough / math.sqrt(NB)
    return (values * factor[:, None, None]).astype(jnp.float32)


def block_scale(key, extent, cuts, smallest, top_value):
    gain = 1.0
    for position, shards_of in cuts:
        steps = jax.random.uniform(jax.random.fold_in(jax.random.fold_in(key, 6), position), (shards_of,), jnp.float32, smallest / len(cuts), top_value / len(cuts))
        gain = gain * jnp.repeat(jnp.exp(steps), extent[position] // shards_of).reshape((-1,) + (1,) * (len(extent) - 1 - position))
    return gain


def normal_values(rng, shape, scale, limit, shards=(), held_as=jnp.bfloat16):
    values = jax.random.normal(rng, shape, jnp.float32) * scale
    if len(shards) > 0:
        values = block_scale(rng, shape, shards, -0.22, 0.18) * values
    return jnp.clip(values, min=-limit, max=limit).astype(held_as)


def setup_inputs(seed: int = 0) -> dict:
    streams_of = jax.random.split(jax.random.key(seed), 7)
    return {
        "rhs_panel": normal_values(streams_of[0], (NB, 2, R), 1.0, 6.0, ((0, 32),), jnp.float32),
        "pivots": jax.random.permutation(streams_of[1], NB).astype(jnp.int32),
        "diag_inverse": draw_diag_inverse(jax.random.fold_in(streams_of[6], 71), 0),
        "panel_column": normal_values(streams_of[3], (ROWS, 2, NB), (2 * NB) ** -0.5, 0.09375, ((0, 8), (2, 4)), jnp.float32),
        "trailing": normal_values(streams_of[4], (ROWS, 2, R), 1.0, 6.0, ((0, 32),), jnp.float32),
        "derivative": draw_derivative(jax.random.fold_in(streams_of[6], 71), 0),
    }


def complex_product(lhs, rhs):
    count_rows = lhs.shape[0]
    inner = lhs.shape[2]
    flat = lhs.reshape(count_rows, 2 * inner)
    real_part = rhs[:, 0, :]
    imag_part = rhs[:, 1, :]
    stacked = jnp.concatenate([jnp.concatenate([real_part, imag_part], axis=1), jnp.concatenate([-imag_part, real_part], axis=1)], axis=0)
    result = jnp.dot(flat, stacked, preferred_element_type=jnp.float32, precision=lax.Precision.HIGHEST)
    return result.reshape(count_rows, 2, rhs.shape[2])


def reference(rhs_panel, pivots, diag_inverse, panel_column, trailing, derivative):
    ordered = jnp.take(rhs_panel, pivots, axis=0)
    adjoint_panel = complex_product(diag_inverse, ordered)
    updated = trailing - complex_product(panel_column, adjoint_panel)
    sensitivity = -jnp.sum(adjoint_panel * derivative, axis=(0, 1))
    return updated, adjoint_panel, sensitivity
```

```python
import functools

import jax
import jax.numpy as jnp
from jax import lax
from jax.experimental import pallas as pl
from jax.experimental.pallas import tpu as pltpu
from jax.sharding import Mesh
from jax.sharding import PartitionSpec as P

F32 = jnp.float32
BF16 = jnp.bfloat16
LANES = 128
MIB = 1 << 20

SMEM = pl.BlockSpec(memory_space=pltpu.SMEM)
VMEM = pl.BlockSpec(memory_space=pltpu.VMEM)
ANY = pl.BlockSpec(memory_space=pl.ANY)
HBM = pl.BlockSpec(memory_space=pltpu.HBM)
PITCH = 40
LONG = (1 << 33, 1 << 20)
OTHERS = (3, 1, 2)
SHIFTS = (0, 1, 3, 2)
sds = jax.ShapeDtypeStruct


def to_rows(x):
    a, b, c = x.shape
    tiles = c // LANES
    return x.reshape(a, b, tiles, LANES).transpose(0, 2, 1, 3).reshape(a * tiles * b, LANES)


def from_rows(x, a, b, c):
    tiles = c // LANES
    return x.reshape(a, tiles, b, LANES).transpose(0, 2, 1, 3).reshape(a, b, c)


def left_half(shape):
    return lax.broadcasted_iota(jnp.int32, shape, 1) < 64


def other_half(x):
    return pltpu.roll(x, 64, 1)


def split(x):
    high = x.astype(BF16)
    low = (x - high.astype(F32)).astype(BF16)
    return high, low


def here(axis):
    return lax.axis_index(axis)


def pack_kernel(rhs_ref, o0, o1, o2, o3, blocks_ref):
    for j in range(2):
        re = rhs_ref[pl.ds(2 * j, 64, stride=4), :]
        im = rhs_ref[pl.ds(2 * j + 1, 64, stride=4), :]
        first = left_half(re.shape)
        blocks_ref[2 * j] = jnp.where(first, re, other_half(im))
        blocks_ref[2 * j + 1] = jnp.where(first, other_half(re), im)
    for d, out in enumerate((o0, o1, o2, o3)):
        out[...] = blocks_ref[lax.bitwise_xor(here("chip"), d)]


def chunk_kernel(after_ref, b0, b3, b1, b2, out_ref):
    del after_ref
    for d, block in enumerate((b0, b1, b2, b3)):
        at = pl.multiple_of(lax.bitwise_xor(here("chip"), d) * 64, 64)
        out_ref[pl.ds(at, 64), :] = block[...]


def diag_copies(first, d_ref, held_ref, sems):
    copies = []
    for i in range(2):
        source = pl.multiple_of(here("core") * 256 + first + i * 64, 64)
        target = held_ref.at[pl.ds(i * 64, 64), pl.ds(0, 32)]
        copies.append(pltpu.make_async_copy(d_ref.at[pl.ds(source, 64)], target, sems.at[i]))
        copies[i].start()
    return copies


def diag_split(copies, held_ref, parts_ref):
    flat_ref = held_ref.reshape(128 * PITCH, LANES)
    for i, copy in enumerate(copies):
        copy.wait()
        for j in range(16):
            for c in range(2):
                x = flat_ref[pl.ds(i * 64 * PITCH + 2 * j + c, 64, stride=PITCH), :]
                for e, part in enumerate(split(x)):
                    row = c * 256 + e * 128 + i * 64
                    parts_ref[row : row + 64, j * LANES : (j + 1) * LANES] = part


def diag_kernel(d_ref, parts_ref, held_ref, sems):
    diag_split(diag_copies(0, d_ref, held_ref, sems), held_ref, parts_ref)


def diag_inverse_kernel(pivots_hbm, d_ref, m0, parts_ref, inverse_ref, part_ref, held_ref, sems, pivots_ref, sem):
    pivots_copy = pltpu.make_async_copy(pivots_hbm, pivots_ref, sem)
    pivots_copy.start()
    copies = diag_copies(128, d_ref, held_ref, sems)
    pivots_copy.wait()

    def invert(step, _):
        for e in range(16):
            i = step * 16 + e
            inverse_ref[pivots_ref[i]] = i
        return 0

    lax.fori_loop(0, 128, invert, 0)
    scatter_rows(inverse_ref, m0, here("core"), SHIFTS[0], part_ref)
    diag_split(copies, held_ref, parts_ref)


def panel_kernel(x_ref, derivative_ref, high_ref, low_ref, packed_ref):
    for j in range(4):
        for c in range(2):
            high, low = split(x_ref[pl.ds(2 * j + c, 256, stride=8), :])
            high_ref[c, :, j * LANES : (j + 1) * LANES] = high
            low_ref[c, :, j * LANES : (j + 1) * LANES] = low
    for j in range(2):
        re = derivative_ref[pl.ds(2 * j, 512, stride=4), :]
        im = derivative_ref[pl.ds(2 * j + 1, 512, stride=4), :]
        first = left_half(re.shape)
        packed_ref[2 * j] = jnp.where(first, re, other_half(im))
        packed_ref[2 * j + 1] = jnp.where(first, other_half(re), im)


def scatter_rows(inverse_ref, chunk, core, t, ordered_ref):
    z = lax.rem(here("pcol") - t + 4, 4)

    def body(step, _):
        first = lax.div(step, 4) * 512 + lax.rem(step, 4) * 16 + core * 256 + z * 64
        for e in range(16):
            ordered_ref[inverse_ref[first + e]] = chunk[step * 16 + e]
        return 0

    lax.fori_loop(0, 16, body, 0)


def fetch(*copies):
    copies = [pltpu.make_async_copy(*copy) for copy in copies]
    for copy in copies:
        copy.start()
    for copy in copies:
        copy.wait()


def relay_kernel(after_ref, x_ref, out_ref):
    del after_ref
    out_ref[...] = x_ref[...]


def bundle_kernel(after_ref, a_ref, b_ref, out_ref):
    del after_ref
    out_ref[0:256, :] = a_ref[...]
    out_ref[256:512, :] = b_ref[...]


def scatter_kernel(names, inverse_hbm, part_hbm, *rest):
    *operands, out_ref, inverse_ref, sem, part_sem = rest
    fetch((inverse_hbm, inverse_ref, sem), (part_hbm, out_ref, part_sem))
    for chunks, operand in zip(names, operands):
        for i, (c, t) in enumerate(chunks):
            chunk = operand.at[i * 256 : (i + 1) * 256]
            scatter_rows(inverse_ref, chunk, lax.bitwise_xor(here("core"), c), t, out_ref)


def solve_kernel(ordered_ref, first_ref, second_ref, out_ref):
    weights = jnp.concatenate(split(ordered_ref[...]), axis=1)
    for i, parts_ref in enumerate((first_ref, second_ref)):
        f = jnp.dot(parts_ref[...], weights, preferred_element_type=F32)
        f = f[:, :LANES] + f[:, LANES:]
        re, im = f[0:128] + f[128:256], f[256:384] + f[384:512]
        cross = other_half(im)
        out_ref[i * 128 : (i + 1) * 128, :] = re + jnp.where(left_half(cross.shape), -cross, cross)


def half_product(members, h, xs, panel_refs, split_refs):
    ph_ref, pl_ref, derivative_ref = panel_refs
    sh_ref, sl_ref = split_refs
    at = pl.multiple_of(lax.bitwise_xor(here("core"), h) * 256, 256)
    row = lax.broadcasted_iota(jnp.int32, (8, LANES), 0)
    tail = jnp.zeros((8, LANES), F32)
    for i, (d, x) in enumerate(zip(members, xs)):
        chip = lax.bitwise_xor(here("chip"), d)
        total = jnp.sum((x * derivative_ref[chip, pl.ds(at, 256), :]).reshape(32, 8, LANES), axis=0)
        tail = jnp.where(row == i, jnp.sum(total, axis=0, keepdims=True), tail)
        columns = slice(i * LANES, (i + 1) * LANES)
        sh_ref[:, columns], sl_ref[:, columns] = split(x)
    f = []
    for c in range(2):
        high, low = ph_ref[c, :, pl.ds(at, 256)], pl_ref[c, :, pl.ds(at, 256)]
        x = jnp.dot(high, sh_ref[...], preferred_element_type=F32)
        x += jnp.dot(high, sl_ref[...], preferred_element_type=F32)
        f.append(x + jnp.dot(low, sh_ref[...], preferred_element_type=F32))
    return f, tail


def half_kernel(members, ph_ref, pl_ref, derivative_ref, *rest):
    *blocks, f_ref, tail_ref, sh_ref, sl_ref = rest
    xs = [block[...] for block in blocks]
    f, tail_ref[...] = half_product(members, 0, xs, (ph_ref, pl_ref, derivative_ref), (sh_ref, sl_ref))
    f_ref[0], f_ref[1] = f


def rest_kernel(members, ph_ref, pl_ref, derivative_ref, f_ref, tail_ref, theirs_ref, *rest):
    *outs, sh_ref, sl_ref, corr_ref = rest[-7:]
    count = len(members)
    xs = [theirs_ref[i * 256 : (i + 1) * 256, :] for i in range(count)]
    f, tail = half_product(members, 1, xs, (ph_ref, pl_ref, derivative_ref), (sh_ref, sl_ref))
    f = [f[0] + f_ref[0], f[1] + f_ref[1]]
    tail += tail_ref[...]
    for out in outs:
        out[count * 64 : count * 64 + 8, :] = tail
    for i in range(count):
        columns = slice(i * LANES, (i + 1) * LANES)
        cross = other_half(f[1][:, columns])
        corr_ref[i] = f[0][:, columns] + jnp.where(left_half(cross.shape), -cross, cross)
        for t, out in enumerate(outs):
            base = pl.multiple_of(lax.rem(here("pcol") + t, 4) * 64, 64)
            out[i * 64 : (i + 1) * 64, :] = corr_ref[i, pl.ds(base, 64), :]


def forward_kernel(after_ref, b0, b1, b2, out_ref):
    del after_ref
    for i, block in enumerate((b0, b1, b2)):
        out_ref[i * 256 : (i + 1) * 256, :] = block[...]


def store_tiles(held_ref, out_ref, first_row, count):
    for j in range(2):
        a, b = held_ref[2 * j], held_ref[2 * j + 1]
        first = left_half(a.shape)
        out_ref[pl.ds(first_row + 2 * j, count, stride=4), :] = jnp.where(first, a, other_half(b))
        out_ref[pl.ds(first_row + 2 * j + 1, count, stride=4), :] = jnp.where(first, other_half(a), b)


def adjoint_kernel(m0, m1, m2, m3, own_ref, others_ref, adjoint_ref, held_ref):
    core = here("core")
    for c in range(2):
        for d, block in enumerate((m0, m1, m2, m3)):
            if c == 1:
                i = OTHERS.index(d) if d else 0
                block = others_ref.at[i * 256 : (i + 1) * 256, :] if d else own_ref
            held_ref[lax.bitwise_xor(here("chip"), d)] = block[...]
        store_tiles(held_ref, adjoint_ref, pl.multiple_of(lax.bitwise_xor(core, c) * 1024, 1024), 256)


def sum_kernel(count, i0, i1, i2, i3, rows_ref, sums_ref, tails_ref):
    pieces = (i0, i1, i2, i3)
    rows = slice(0, count * 64)
    rows_ref[...] = (i0[rows, :] + i1[rows, :]) + (i2[rows, :] + i3[rows, :])
    for t, piece in enumerate(pieces):
        tails_ref[lax.rem(here("pcol") - t + 4, 4)] = piece[count * 64 : count * 64 + 8, :]
    value = -((tails_ref[0] + tails_ref[1]) + (tails_ref[2] + tails_ref[3]))
    sums_ref[...] = value + other_half(value)


def final_kernel(
    trailing_ref, own_rows, own_sums, b0, b1, b2, b3, updated_ref, sensitivity_ref,
    rows_ref, group_ref, tails_ref, held_ref, sums_ref,
):
    sum_kernel(3, b0, b1, b2, b3, rows_ref, group_ref, tails_ref)
    for d in range(4):
        chip = lax.bitwise_xor(here("chip"), d)
        i = OTHERS.index(d) if d else 0
        rows = rows_ref[i * 64 : (i + 1) * 64, :] if d else own_rows[...]
        sums = group_ref[i : i + 1, :] if d else own_sums[0:1, :]
        held_ref[chip] = rows
        sums_ref[chip] = sums
    for j in range(2):
        a, b = held_ref[2 * j], held_ref[2 * j + 1]
        first = left_half(a.shape)
        at = pl.ds(2 * j, 64, stride=4)
        updated_ref[at, :] = trailing_ref[at, :] - jnp.where(first, a, other_half(b))
        at = pl.ds(2 * j + 1, 64, stride=4)
        updated_ref[at, :] = trailing_ref[at, :] - jnp.where(first, other_half(a), b)
        sensitivity_ref[j : j + 1, :] = jnp.where(left_half((1, LANES)), sums_ref[2 * j], sums_ref[2 * j + 1])


def crossed(x, axis, count, d):
    return lax.ppermute(x, axis, [(i, i ^ d) for i in range(count)])


def shifted(x, axis, count, t):
    return lax.ppermute(x, axis, [(i, (i + t) % count) for i in range(count)])


def call(kernel, operands, in_specs, outs, scratch=(), mib=4, cost=None):
    return pl.pallas_call(
        kernel,
        in_specs=in_specs,
        out_specs=[SMEM if o.dtype == jnp.int32 else VMEM for o in outs],
        out_shape=outs,
        scratch_shapes=list(scratch),
        compiler_params=pltpu.CompilerParams(vmem_limit_bytes=mib * MIB),
        cost_estimate=cost and pl.CostEstimate(flops=cost[0], bytes_accessed=cost[1], transcendentals=0),
    )(*operands)


def per_device(rhs_panel, pivots, diag_inverse, panel_column, trailing, derivative):
    def rows(count):
        return sds((count, LANES), F32)

    def buffer(*shape, dtype=F32):
        return pltpu.VMEM(shape, dtype)

    inverse_scratch = [pltpu.SMEM((2048,), jnp.int32), pltpu.SemaphoreType.DMA]

    panel = sds((2, 256, 512), BF16)
    ph, pl_, derivative_packed = call(
        panel_kernel, [to_rows(panel_column), to_rows(derivative)], [VMEM] * 2,
        [panel, panel, sds((4, 512, LANES), F32)], cost=(1 << 21, 4 << 20),
    )

    half = sds((512, 2048), BF16)
    diagonal_rows = to_rows(diag_inverse).reshape(512, 32, LANES)
    held = [buffer(128, PITCH, LANES), pltpu.SemaphoreType.DMA((2,))]
    (first_half,) = call(diag_kernel, [diagonal_rows], [HBM], [half], held, mib=48, cost=(1 << 22, 4 << 20))

    packed = call(pack_kernel, [to_rows(rhs_panel)], [VMEM], [rows(64)] * 4, [buffer(4, 64, LANES)], cost=LONG)
    arrived = [crossed(packed[d], "chip", 4, d) for d in (3, 1, 2)]
    (chunk,) = call(chunk_kernel, [first_half, packed[0], *arrived], [ANY] + [VMEM] * 4, [rows(256)], cost=LONG)
    mine = [chunk] + [shifted(chunk, "pcol", 4, t) for t in SHIFTS[1:]]

    def single(x):
        return x.reshape(x.shape[0], 1, LANES)

    def relay(after, x, cost):
        return call(relay_kernel, [after, x], [ANY, VMEM], [rows(x.shape[0])], cost=cost)[0]

    def scatter(part, *named):
        return call(
            functools.partial(scatter_kernel, [n for n, _ in named]),
            [inverse, part, *[single(x) for _, x in named]], [ANY] * 2 + [VMEM] * len(named),
            [ordered], [*inverse_scratch, pltpu.SemaphoreType.DMA], cost=(1 << 20, 1 << 20),
        )[0]

    ordered = sds((2048, 1, LANES), F32)
    second_half, inverse, part = call(
        diag_inverse_kernel, [pivots, diagonal_rows, single(chunk)], [ANY, HBM, VMEM],
        [half, sds((2048,), jnp.int32), ordered], held + inverse_scratch, mib=46, cost=(1 << 22, 4 << 20),
    )
    a, b, c = SHIFTS[1:]
    (bundle,) = call(bundle_kernel, [second_half, chunk, mine[1]], [ANY, VMEM, VMEM], [rows(512)])
    bundle = crossed(bundle, "core", 2, 1)
    second = crossed(mine[2], "core", 2, 1)
    part = scatter(part, ([(0, a)], mine[1]), ([(0, b)], mine[2]))
    last = crossed(relay(part, mine[3], LONG), "core", 2, 1)
    part = scatter(part, ([(0, c)], mine[3]), ([(1, b)], second), ([(1, 0), (1, a)], bundle))
    part = scatter(part, ([(1, c)], last))
    (solved,) = call(solve_kernel, [part.reshape(2048, LANES), first_half, second_half], [VMEM] * 3, [rows(256)], mib=16)

    blocks = {0: solved, **{d: crossed(solved, "chip", 4, d) for d in OTHERS}}
    other_blocks = [blocks[d] for d in OTHERS]
    own_swapped = crossed(solved, "core", 2, 1)

    panels = [ph, pl_, derivative_packed]

    def half_of(members, blocks):
        width = len(members) * LANES
        return call(
            functools.partial(half_kernel, members), [*panels, *blocks], [VMEM] * (3 + len(blocks)),
            [sds((2, 256, width), F32), rows(8)], [buffer(256, width, dtype=BF16)] * 2, mib=8,
            cost=(len(members) * (50 << 20), 2 << 20),
        )

    def rest_of(members, halves, theirs, before=()):
        count = len(members)
        return call(
            functools.partial(rest_kernel, members), [*panels, *halves, theirs, *before],
            [VMEM] * 6 + [ANY] * len(before), [rows(count * 64 + 8)] * 4,
            [buffer(256, count * LANES, dtype=BF16)] * 2 + [buffer(count, 256, LANES)], mib=8,
            cost=(count * (50 << 20), 2 << 20),
        )

    def exchange(pieces):
        return [pieces[0]] + [shifted(pieces[t], "pcol", 4, t) for t in (1, 2, 3)]

    own_pieces = rest_of((0,), half_of((0,), [solved]), own_swapped)
    own_arrived = exchange(own_pieces)
    own_total = call(
        functools.partial(sum_kernel, 1), own_arrived, [VMEM] * 4, [rows(64), rows(8)],
        [buffer(4, 8, LANES)], cost=LONG,
    )
    (forward,) = call(forward_kernel, [own_pieces[0], *other_blocks], [ANY] + [VMEM] * 3, [rows(768)])
    others_swapped = crossed(forward, "core", 2, 1)
    before = [own_total[0]]
    other_pieces = rest_of(OTHERS, half_of(OTHERS, other_blocks), others_swapped, before)

    (adjoint,) = call(
        adjoint_kernel, [*[blocks[d] for d in range(4)], own_swapped, others_swapped], [VMEM] * 6, [rows(2048)], [buffer(4, 256, LANES)],
        mib=6, cost=(1 << 18, 3 << 20),
    )
    updated, sensitivity = call(
        final_kernel, [to_rows(trailing), *own_total, *exchange(other_pieces)], [VMEM] * 7, [rows(256), rows(2)],
        [buffer(192, LANES), buffer(8, LANES), buffer(4, 8, LANES), buffer(4, 64, LANES), buffer(4, 1, LANES)],
    )
    return (
        from_rows(updated, 64, 2, 256),
        from_rows(adjoint, 512, 2, 256),
        sensitivity.reshape(256),
    )


def complex_product(lhs, rhs):
    rows, _, inner = lhs.shape
    re, im = rhs[:, 0, :], rhs[:, 1, :]
    stacked = jnp.concatenate(
        [jnp.concatenate([re, im], axis=1), jnp.concatenate([-im, re], axis=1)], axis=0
    )
    result = jnp.dot(
        lhs.reshape(rows, 2 * inner), stacked, preferred_element_type=F32, precision=lax.Precision.HIGHEST
    )
    return result.reshape(rows, 2, rhs.shape[2])


def per_device_plain(rhs_panel, pivots, diag_inverse, panel_column, trailing, derivative):
    gathered = lax.all_gather(rhs_panel, ("prow", "pcol"), axis=0, tiled=True)
    solved = complex_product(diag_inverse, jnp.take(gathered, pivots, axis=0))
    correction = lax.psum_scatter(
        complex_product(panel_column, solved), "pcol", scatter_dimension=0, tiled=True
    )
    sensitivity = lax.psum(-jnp.sum(solved * derivative, axis=(0, 1)), "pcol")
    return trailing - correction, solved, sensitivity


def solution(mesh):
    fits = mesh.shape["prow"] == 8 and mesh.shape["pcol"] == 4
    if fits:
        mesh = Mesh(mesh.devices.reshape(4, 2, 4), ("chip", "core", "pcol"))
        row = ("chip", "core")
    else:
        row = ("prow",)
    in_specs = (
        P(row + ("pcol",), None, None),
        P(),
        P("pcol", None, None),
        P(row, None, "pcol"),
        P(row + ("pcol",), None, None),
        P("pcol", None, None),
    )
    out_specs = (P(row + ("pcol",), None, None), P("pcol", None, None), P())
    return jax.shard_map(
        per_device if fits else per_device_plain,
        mesh=mesh, in_specs=in_specs, out_specs=out_specs, check_vma=False,
    )
```
